32 devices in a mesh: ia: 16 (over z, x, core), ja: 2 (over y).
Axes of the slice: x: 2, y: 2, z: 4, core: 2. Of those that a mesh axis runs over, the one named last changes fastest.
Arguments:
- position: float32 [3, 8192], P(None, ('ia', 'ja')), may hold values from -5 to 5
- velocity: float32 [3, 8192], P(None, ('ia', 'ja')), may hold values from -4 to 4
- mass: float32 [8192], P(('ia', 'ja')), may hold values from 1.2207031e-05 to 0.0012207031
Outputs:
- final_position: float32 [3, 8192], P(None, ('ia', 'ja'))
- final_velocity: float32 [3, 8192], P(None, ('ia', 'ja'))
- final_accel: float32 [3, 8192], P(None, ('ia', 'ja'))
- final_jerk: float32 [3, 8192], P(None, ('ia', 'ja'))
The draws below stay inside these ranges and needn't reach their ends.
All inputs are finite; a program needn't handle non-finite values.
Results may differ from the reference program's by a relative error of at most 0.00017.
Values sent between devices are 32-bit elements; how exact they have to be, the bound alone decides.
A program may use at most 128 MiB of HBM per device.

```python
import math
import jax
import jax.numpy as jnp
from jax import lax

STEPS = 4
STARS = 8192


def draw_position(key, part):
    key = jax.random.fold_in(key, 11)
    base_key = jax.random.fold_in(key, 0)
    central = 0.3 * jax.random.normal(base_key, (3, STARS), jnp.float32)
    return jnp.clip(central, -5.0, 5.0).astype(jnp.float32)


def block_levels(stream_key, extent, cuts, low, top_value):
    factor_of, own = 1.0, jax.random.fold_in(stream_key, 6)
    for axis_at, blocks in cuts:
        draws = jnp.exp(jax.random.uniform(jax.random.fold_in(own, axis_at), (blocks,), jnp.float32, low / len(cuts), top_value / len(cuts)))
        factor_of = factor_of * jnp.repeat(draws, extent[axis_at] // blocks).reshape([-1 if axis == axis_at else 1 for axis in range(len(extent))])
    return factor_of


def bell_draw(key, dims, scale, most, cuts=(), held_as=jnp.bfloat16):
    factor_of = block_levels(key, dims, cuts, -0.22, 0.18) if cuts else 1.0
    drawn = jax.random.normal(key, dims, jnp.float32) * scale * factor_of
    return jnp.minimum(jnp.maximum(drawn, -most), most).astype(held_as)


def setup_inputs(seed: int = 0) -> dict:
    arg_keys = jax.random.split(jax.random.key(seed), 4)
    return {
        "position": draw_position(jax.random.fold_in(arg_keys[3], 71), 0),
        "velocity": bell_draw(arg_keys[1], (3, STARS), 0.5, 4.0, ((1, 32),), jnp.float32),
        "mass": jnp.clip(jnp.exp(math.log(0.0012207031) - 4.6051702 * jax.random.uniform(arg_keys[2], (STARS,), jnp.float32) ** block_levels(arg_keys[2], (STARS,), ((0, 32),), -0.2, 0.2)), 1.220703143189894e-05, 0.0012207031),
    }


soft_square = 0.0025
time_step = 0.03125

def forces(position, velocity, mass):
    count = position.shape[1]
    width = math.gcd(count, 256)
    blocks_pos = position.reshape(3, count // width, width).transpose(1, 0, 2)
    blocks_vel = velocity.reshape(3, count // width, width).transpose(1, 0, 2)

    def one_block(pair):
        here_pos, here_vel = pair
        offset = position[:, None, :] - here_pos[:, :, None]
        closing = velocity[:, None, :] - here_vel[:, :, None]
        square = lax.optimization_barrier(jnp.sum(offset * offset, 0)) + soft_square
        inverse = lax.rsqrt(square)
        cube = inverse * inverse * inverse
        radial = 3.0 * lax.optimization_barrier(jnp.sum(offset * closing, 0)) / square
        weighted = cube * mass[None, :]
        pull_sum = lax.optimization_barrier(jnp.sum(offset * weighted, 2))
        surge_sum = lax.optimization_barrier(jnp.sum((closing - radial * offset) * weighted, 2))
        return jnp.concatenate([pull_sum, surge_sum], 0)
    result = lax.map(one_block, (blocks_pos, blocks_vel))
    result = result.transpose(1, 0, 2).reshape(6, count)
    return (result[0:3], result[3:6])

def reference(position, velocity, mass):
    accel, jerk = forces(position, velocity, mass)
    step_sq = time_step * time_step
    for step_index in range(STEPS):
        predicted_pos = position + time_step * velocity + step_sq / 2.0 * accel + step_sq * time_step / 6.0 * jerk
        predicted_vel = velocity + time_step * accel + step_sq / 2.0 * jerk
        new_accel, new_jerk = forces(predicted_pos, predicted_vel, mass)
        new_velocity = velocity + time_step / 2.0 * (accel + new_accel) + step_sq / 12.0 * (jerk - new_jerk)
        position = position + time_step / 2.0 * (velocity + new_velocity) + step_sq / 12.0 * (accel - new_accel)
        velocity = new_velocity
        accel = new_accel
        jerk = new_jerk
    return (position, velocity, accel, jerk)
```

```python
import functools

import jax
import jax.numpy as jnp
from jax import lax
from jax.experimental import pallas as pl
from jax.experimental.pallas import tpu as pltpu
from jax.sharding import PartitionSpec as P

STEPS = 4
GROUP = 4
ROWS = 32
LANES = 128

soft_square = 0.0025
time_step = 0.03125

MESH = pl.DeviceIdType.MESH


def round_bf16(x):
    return x.astype(jnp.bfloat16).astype(jnp.float32)


def spread_rows(state, rows_ref):
    n = state.shape[1]
    turned = state.T
    for q in range(6):
        rows_ref[q] = jnp.broadcast_to(turned[:, q : q + 1], (n, LANES))


def source_sides(block):
    mass = block[6:7]
    n = block.shape[1]
    part = lax.broadcasted_iota(jnp.int32, (8, n), 0)
    full = jnp.where(part == 6, mass, block * mass)
    full = jnp.where(part == 7, 0.0, full)
    first = round_bf16(full)
    rest = full - first
    second = round_bf16(rest)
    third = rest - second
    stacked = jnp.concatenate([first, second, third, jnp.zeros_like(full)], 0)
    return stacked.astype(jnp.bfloat16)


def pair_tiles(block_ref, rows_ref, w_ref, v_ref, side_ref, slots, own):
    n = rows_ref.shape[1]
    depth = slots * n
    for k in range(slots):
        side = source_sides(block_ref[k])
        side_ref[:, k * n : (k + 1) * n] = side
        side_ref[:, depth + k * n : depth + (k + 1) * n] = side

    def row_tile(r, carry):
        start = pl.multiple_of(r * ROWS, ROWS)
        here = [rows_ref[q, pl.ds(start, ROWS), :] for q in range(6)]
        for k in range(slots):
            for c in range(n // LANES):
                lanes = slice(c * LANES, (c + 1) * LANES)
                there = [block_ref[k, q : q + 1, lanes] for q in range(6)]
                off = [there[q] - here[q] for q in range(3)]
                clo = [there[q + 3] - here[q + 3] for q in range(3)]
                square = off[0] * off[0] + off[1] * off[1] + (off[2] * off[2] + soft_square)
                dot = off[0] * clo[0] + off[1] * clo[1] + off[2] * clo[2]
                inverse = lax.rsqrt(square)
                inv2 = inverse * inverse
                w = inv2 * inverse
                if own and k == 0:
                    row_at = lax.broadcasted_iota(jnp.int32, (ROWS, LANES), 0) + start
                    col_at = lax.broadcasted_iota(jnp.int32, (ROWS, LANES), 1) + c * LANES
                    w = jnp.where(row_at == col_at, 0.0, w)
                v = w * (inv2 * dot)
                at = k * n + c * LANES
                for ref, val in ((w_ref, w), (v_ref, v)):
                    high = val.astype(jnp.bfloat16)
                    low = (val - high.astype(jnp.float32)).astype(jnp.bfloat16)
                    ref[pl.ds(start, ROWS), at : at + LANES] = high
                    ref[pl.ds(start, ROWS), depth + at : depth + at + LANES] = low
        return carry

    lax.fori_loop(0, n // ROWS, row_tile, 0)


def contract(side_ref, pair_ref):
    return lax.dot_general(
        side_ref[...], pair_ref[...], (((1,), (1,)), ((), ())), preferred_element_type=jnp.float32
    )


def fold(total):
    return total[0:8] + total[8:16] + total[16:24]


def finish(state, w_sum, v_sum):
    pos, vel = state[0:3], state[3:6]
    ws, vs = fold(w_sum), fold(v_sum)
    accel = ws[0:3] - pos * ws[6:7]
    jerk = (ws[3:6] - vel * ws[6:7]) - 3.0 * (vs[0:3] - pos * vs[6:7])
    return accel, jerk


def kernel(
    axes, sizes, pos_ref, vel_ref, mass_ref, opos_ref, ovel_ref, oacc_ref, ojerk_ref,
    gath, rows, w_buf, v_buf, side, w_sum, v_sum, send_sem, recv_sem,
):
    nia, nja = sizes
    devices = nia * nja
    slots = min(GROUP, devices)
    groups = devices // slots
    ia, ja = lax.axis_index(axes[0]), lax.axis_index(axes[1])

    def partner(t):
        return ((ia + t // nja) % nia, (ja + t % nja) % nja)

    barrier = pltpu.get_barrier_semaphore()

    def greet(t, carry):
        pl.semaphore_signal(barrier, inc=1, device_id=partner(t), device_id_type=MESH)
        return carry

    lax.fori_loop(1, devices, greet, 0)
    pl.semaphore_wait(barrier, devices - 1)

    def copy(par, t):
        return pltpu.make_async_remote_copy(
            src_ref=gath.at[par, 0],
            dst_ref=gath.at[par, t],
            send_sem=send_sem.at[par, t],
            recv_sem=recv_sem.at[par, t],
            device_id=partner(t),
            device_id_type=MESH,
        )

    def forces(par, pos, vel):
        state = jnp.concatenate([pos, vel, mass_ref[...], jnp.zeros_like(mass_ref)], 0)
        gath[par, 0] = state

        def begin(t, carry):
            copy(par, t).start()
            return carry

        lax.fori_loop(1, devices, begin, 0)
        spread_rows(state, rows)
        w_sum[...] = jnp.zeros_like(w_sum)
        v_sum[...] = jnp.zeros_like(v_sum)

        def group(g, own):
            start = g * slots
            for k in range(slots):
                if not (own and k == 0):
                    copy(par, start + k).wait_recv()
            pair_tiles(gath.at[par, pl.ds(start, slots)], rows, w_buf, v_buf, side, slots, own)
            w_sum[...] += contract(side, w_buf)
            v_sum[...] += contract(side, v_buf)

        group(0, True)

        def later(g, carry):
            group(g, False)
            return carry

        lax.fori_loop(1, groups, later, 0)

        def finish_send(t, carry):
            copy(par, t).wait_send()
            return carry

        lax.fori_loop(1, devices, finish_send, 0)
        return finish(state, w_sum[...], v_sum[...])

    pos, vel = pos_ref[...], vel_ref[...]
    step_sq = time_step * time_step
    accel, jerk = forces(0, pos, vel)
    opos_ref[...] = pos
    ovel_ref[...] = vel
    oacc_ref[...] = accel
    ojerk_ref[...] = jerk

    def step(index, carry):
        position, velocity = opos_ref[...], ovel_ref[...]
        accel, jerk = oacc_ref[...], ojerk_ref[...]
        predicted_pos = (
            position
            + time_step * velocity
            + step_sq / 2.0 * accel
            + step_sq * time_step / 6.0 * jerk
        )
        predicted_vel = velocity + time_step * accel + step_sq / 2.0 * jerk
        new_accel, new_jerk = forces((index + 1) % 2, predicted_pos, predicted_vel)
        new_velocity = (
            velocity + time_step / 2.0 * (accel + new_accel) + step_sq / 12.0 * (jerk - new_jerk)
        )
        opos_ref[...] = (
            position
            + time_step / 2.0 * (velocity + new_velocity)
            + step_sq / 12.0 * (accel - new_accel)
        )
        ovel_ref[...] = new_velocity
        oacc_ref[...] = new_accel
        ojerk_ref[...] = new_jerk
        return carry

    lax.fori_loop(0, STEPS, step, 0)


def per_device(axes, sizes, position, velocity, mass):
    n = position.shape[1]
    devices = sizes[0] * sizes[1]
    depth = 2 * min(GROUP, devices) * n
    vmem = pl.BlockSpec(memory_space=pltpu.VMEM)
    shape = jax.ShapeDtypeStruct(position.shape, jnp.float32)
    return tuple(
        pl.pallas_call(
            functools.partial(kernel, axes, sizes),
            out_shape=(shape,) * 4,
            in_specs=[vmem] * 3,
            out_specs=(vmem,) * 4,
            scratch_shapes=[
                pltpu.VMEM((2, devices, 8, n), jnp.float32),
                pltpu.VMEM((6, n, LANES), jnp.float32),
                pltpu.VMEM((n, depth), jnp.bfloat16),
                pltpu.VMEM((n, depth), jnp.bfloat16),
                pltpu.VMEM((32, depth), jnp.bfloat16),
                pltpu.VMEM((32, n), jnp.float32),
                pltpu.VMEM((32, n), jnp.float32),
                pltpu.SemaphoreType.DMA((2, devices)),
                pltpu.SemaphoreType.DMA((2, devices)),
            ],
            compiler_params=pltpu.CompilerParams(
                collective_id=0, has_side_effects=True, vmem_limit_bytes=40 * 1024 * 1024
            ),
        )(position, velocity, mass[None, :])
    )


def solution(mesh):
    axes = ("ia", "ja")
    sizes = (mesh.shape["ia"], mesh.shape["ja"])
    split = P(None, axes)
    return jax.shard_map(
        functools.partial(per_device, axes, sizes),
        mesh=mesh,
        in_specs=(split, split, P(axes)),
        out_specs=(split,) * 4,
        check_vma=False,
    )
```

```python
import functools

import jax
import jax.numpy as jnp
from jax import lax
from jax.experimental import pallas as pl
from jax.experimental.pallas import tpu as pltpu
from jax.sharding import PartitionSpec as P

STEPS = 4
GROUP = 4
ROWS = 256
LANES = 128

soft_square = 0.0025
time_step = 0.03125

MESH = pl.DeviceIdType.MESH


def round_bf16(x):
    return x.astype(jnp.bfloat16).astype(jnp.float32)


def spread_rows(state, rows_ref):
    n = state.shape[1]
    turned = state.T
    for q in range(6):
        rows_ref[q] = jnp.broadcast_to(turned[:, q : q + 1], (n, LANES))


def source_sides(block):
    mass = block[6:7]
    n = block.shape[1]
    part = lax.broadcasted_iota(jnp.int32, (8, n), 0)
    full = jnp.where(part == 6, mass, block * mass)
    full = jnp.where(part == 7, 0.0, full)
    first = round_bf16(full)
    rest = full - first
    second = round_bf16(rest)
    third = rest - second
    stacked = jnp.concatenate([first, second, third, jnp.zeros_like(full)], 0)
    return stacked.astype(jnp.bfloat16)


def pair_tiles(block_ref, rows_ref, pair_ref, side_ref, slots, own):
    n = rows_ref.shape[1]
    depth = slots * n
    for k in range(slots):
        side = source_sides(block_ref[k])
        side_ref[:, k * n : (k + 1) * n] = side
        side_ref[:, depth + k * n : depth + (k + 1) * n] = side

    def row_tile(r, carry):
        start = pl.multiple_of(r * ROWS, ROWS)
        here = [rows_ref[q, pl.ds(start, ROWS), :] for q in range(6)]
        tiles = [[], [], [], []]
        for k in range(slots):
            for c in range(n // LANES):
                lanes = slice(c * LANES, (c + 1) * LANES)
                there = [block_ref[k, q : q + 1, lanes] for q in range(6)]
                off = [there[q] - here[q] for q in range(3)]
                clo = [there[q + 3] - here[q + 3] for q in range(3)]
                square = off[0] * off[0] + off[1] * off[1] + (off[2] * off[2] + soft_square)
                dot = off[0] * clo[0] + off[1] * clo[1] + off[2] * clo[2]
                inverse = lax.rsqrt(square)
                inv2 = inverse * inverse
                w = inv2 * inverse
                if own and k == 0:
                    row_at = lax.broadcasted_iota(jnp.int32, (ROWS, LANES), 0) + start
                    col_at = lax.broadcasted_iota(jnp.int32, (ROWS, LANES), 1) + c * LANES
                    w = jnp.where(row_at == col_at, 0.0, w)
                v = w * (inv2 * dot)
                for at, val in ((0, w), (2, v)):
                    high = val.astype(jnp.bfloat16)
                    tiles[at].append(high)
                    tiles[at + 1].append((val - high.astype(jnp.float32)).astype(jnp.bfloat16))
        for at in range(2):
            high = jnp.concatenate(tiles[2 * at], 1)
            low = jnp.concatenate(tiles[2 * at + 1], 1)
            both = jnp.concatenate([high, low], 1)
            got = lax.dot_general(both, side_ref[...], (((1,), (1,)), ((), ())), preferred_element_type=jnp.float32)
            pair_ref[pl.ds(start + at * n, ROWS), :] += got
        return carry

    lax.fori_loop(0, n // ROWS, row_tile, 0)


def fold(total):
    return total[0:8] + total[8:16] + total[16:24]


def finish(state, w_sum, v_sum):
    pos, vel = state[0:3], state[3:6]
    ws, vs = fold(w_sum), fold(v_sum)
    accel = ws[0:3] - pos * ws[6:7]
    jerk = (ws[3:6] - vel * ws[6:7]) - 3.0 * (vs[0:3] - pos * vs[6:7])
    return accel, jerk


def kernel(
    axes, sizes, pos_ref, vel_ref, mass_ref, opos_ref, ovel_ref, oacc_ref, ojerk_ref,
    gath, rows, side, sums, send_sem, recv_sem,
):
    nia, nja = sizes
    devices = nia * nja
    slots = min(GROUP, devices)
    groups = devices // slots
    ia, ja = lax.axis_index(axes[0]), lax.axis_index(axes[1])

    def partner(t):
        return ((ia + t // nja) % nia, (ja + t % nja) % nja)

    barrier = pltpu.get_barrier_semaphore()

    def greet(t, carry):
        pl.semaphore_signal(barrier, inc=1, device_id=partner(t), device_id_type=MESH)
        return carry

    lax.fori_loop(1, devices, greet, 0)
    pl.semaphore_wait(barrier, devices - 1)

    def copy(par, t):
        return pltpu.make_async_remote_copy(
            src_ref=gath.at[par, 0],
            dst_ref=gath.at[par, t],
            send_sem=send_sem.at[par, t],
            recv_sem=recv_sem.at[par, t],
            device_id=partner(t),
            device_id_type=MESH,
        )

    def forces(par, pos, vel):
        state = jnp.concatenate([pos, vel, mass_ref[...], jnp.zeros_like(mass_ref)], 0)
        gath[par, 0] = state

        def begin(t, carry):
            copy(par, t).start()
            return carry

        lax.fori_loop(1, devices, begin, 0)
        spread_rows(state, rows)
        sums[...] = jnp.zeros_like(sums)

        def group(g, own):
            start = g * slots
            for k in range(slots):
                if not (own and k == 0):
                    copy(par, start + k).wait_recv()
            pair_tiles(gath.at[par, pl.ds(start, slots)], rows, sums, side, slots, own)

        group(0, True)

        def later(g, carry):
            group(g, False)
            return carry

        lax.fori_loop(1, groups, later, 0)

        def finish_send(t, carry):
            copy(par, t).wait_send()
            return carry

        lax.fori_loop(1, devices, finish_send, 0)
        return finish(state, sums[: pos.shape[1], :].T, sums[pos.shape[1] :, :].T)

    pos, vel = pos_ref[...], vel_ref[...]
    step_sq = time_step * time_step
    accel, jerk = forces(0, pos, vel)
    opos_ref[...] = pos
    ovel_ref[...] = vel
    oacc_ref[...] = accel
    ojerk_ref[...] = jerk

    def step(index, carry):
        position, velocity = opos_ref[...], ovel_ref[...]
        accel, jerk = oacc_ref[...], ojerk_ref[...]
        predicted_pos = (
            position
            + time_step * velocity
            + step_sq / 2.0 * accel
            + step_sq * time_step / 6.0 * jerk
        )
        predicted_vel = velocity + time_step * accel + step_sq / 2.0 * jerk
        new_accel, new_jerk = forces((index + 1) % 2, predicted_pos, predicted_vel)
        new_velocity = (
            velocity + time_step / 2.0 * (accel + new_accel) + step_sq / 12.0 * (jerk - new_jerk)
        )
        opos_ref[...] = (
            position
            + time_step / 2.0 * (velocity + new_velocity)
            + step_sq / 12.0 * (accel - new_accel)
        )
        ovel_ref[...] = new_velocity
        oacc_ref[...] = new_accel
        ojerk_ref[...] = new_jerk
        return carry

    lax.fori_loop(0, STEPS, step, 0)


def per_device(axes, sizes, position, velocity, mass):
    n = position.shape[1]
    devices = sizes[0] * sizes[1]
    depth = 2 * min(GROUP, devices) * n
    vmem = pl.BlockSpec(memory_space=pltpu.VMEM)
    shape = jax.ShapeDtypeStruct(position.shape, jnp.float32)
    return tuple(
        pl.pallas_call(
            functools.partial(kernel, axes, sizes),
            out_shape=(shape,) * 4,
            in_specs=[vmem] * 3,
            out_specs=(vmem,) * 4,
            scratch_shapes=[
                pltpu.VMEM((2, devices, 8, n), jnp.float32),
                pltpu.VMEM((6, n, LANES), jnp.float32),
                pltpu.VMEM((32, depth), jnp.bfloat16),
                pltpu.VMEM((2 * n, 32), jnp.float32),
                pltpu.SemaphoreType.DMA((2, devices)),
                pltpu.SemaphoreType.DMA((2, devices)),
            ],
            compiler_params=pltpu.CompilerParams(
                collective_id=0, has_side_effects=True, vmem_limit_bytes=40 * 1024 * 1024
            ),
        )(position, velocity, mass[None, :])
    )


def solution(mesh):
    axes = ("ia", "ja")
    sizes = (mesh.shape["ia"], mesh.shape["ja"])
    split = P(None, axes)
    return jax.shard_map(
        functools.partial(per_device, axes, sizes),
        mesh=mesh,
        in_specs=(split, split, P(axes)),
        out_specs=(split,) * 4,
        check_vma=False,
    )
```

```python
import functools

import jax
import jax.numpy as jnp
from jax import lax
from jax.experimental import pallas as pl
from jax.experimental.pallas import tpu as pltpu
from jax.sharding import PartitionSpec as P

STEPS = 4
GROUP = 4
LANES = 128

soft_square = 0.0025
time_step = 0.03125

MESH = pl.DeviceIdType.MESH


def round_bf16(x):
    return x.astype(jnp.bfloat16).astype(jnp.float32)


def spread_rows(state, rows_ref):
    n = state.shape[1]
    turned = state.T
    for q in range(6):
        rows_ref[q] = jnp.broadcast_to(turned[:, q : q + 1], (n, LANES))


def source_sides(block):
    mass = block[6:7]
    n = block.shape[1]
    part = lax.broadcasted_iota(jnp.int32, (8, n), 0)
    full = jnp.where(part == 6, mass, block * mass)
    full = jnp.where(part == 7, 0.0, full)
    first = round_bf16(full)
    rest = full - first
    second = round_bf16(rest)
    third = rest - second
    stacked = jnp.concatenate([first, second, third, jnp.zeros_like(full)], 0)
    return stacked.astype(jnp.bfloat16)


def pair_tiles(block_ref, rows_ref, pair_ref, side_ref, slots, own, arrive):
    n = rows_ref.shape[1]
    depth = slots * n
    ROWS = n

    def prepare(k):
        side = source_sides(block_ref[k])
        side_ref[:, k * n : (k + 1) * n] = side
        side_ref[:, depth + k * n : depth + (k + 1) * n] = side

    if not own:
        for k in range(slots):
            prepare(k)

    def row_tile(r, carry):
        start = r * ROWS
        here = [rows_ref[q, pl.ds(start, ROWS), :] for q in range(6)]
        tiles = [[], [], [], []]
        for k in range(slots):
            if own:
                arrive(k)
                prepare(k)
            for c in range(n // LANES):
                lanes = slice(c * LANES, (c + 1) * LANES)
                there = [block_ref[k, q : q + 1, lanes] for q in range(6)]
                off = [there[q] - here[q] for q in range(3)]
                clo = [there[q + 3] - here[q + 3] for q in range(3)]
                square = off[0] * off[0] + off[1] * off[1] + (off[2] * off[2] + soft_square)
                dot = off[0] * clo[0] + off[1] * clo[1] + off[2] * clo[2]
                inverse = lax.rsqrt(square)
                inv2 = inverse * inverse
                w = inv2 * inverse
                if own and k == 0:
                    row_at = lax.broadcasted_iota(jnp.int32, (ROWS, LANES), 0) + start
                    col_at = lax.broadcasted_iota(jnp.int32, (ROWS, LANES), 1) + c * LANES
                    w = jnp.where(row_at == col_at, 0.0, w)
                v = w * (inv2 * dot)
                for at, val in ((0, w), (2, v)):
                    high = val.astype(jnp.bfloat16)
                    tiles[at].append(high)
                    tiles[at + 1].append((val - high.astype(jnp.float32)).astype(jnp.bfloat16))
        for at in range(2):
            high = jnp.concatenate(tiles[2 * at], 1)
            low = jnp.concatenate(tiles[2 * at + 1], 1)
            both = jnp.concatenate([high, low], 1)
            got = lax.dot_general(both, side_ref[...], (((1,), (1,)), ((), ())), preferred_element_type=jnp.float32)
            pair_ref[pl.ds(start + at * n, ROWS), :] += got
        return carry

    row_tile(0, 0)


def fold(total):
    return total[0:8] + total[8:16] + total[16:24]


def finish(state, w_sum, v_sum):
    pos, vel = state[0:3], state[3:6]
    ws, vs = fold(w_sum), fold(v_sum)
    accel = ws[0:3] - pos * ws[6:7]
    jerk = (ws[3:6] - vel * ws[6:7]) - 3.0 * (vs[0:3] - pos * vs[6:7])
    return accel, jerk


def kernel(
    axes, sizes, pos_ref, vel_ref, mass_ref, opos_ref, ovel_ref, oacc_ref, ojerk_ref,
    gath, rows, side, sums, send_sem, recv_sem,
):
    nia, nja = sizes
    devices = nia * nja
    slots = min(GROUP, devices)
    groups = devices // slots
    ia, ja = lax.axis_index(axes[0]), lax.axis_index(axes[1])

    def partner(t):
        return ((ia + t // nja) % nia, (ja + t % nja) % nja)

    barrier = pltpu.get_barrier_semaphore()

    def greet(t, carry):
        pl.semaphore_signal(barrier, inc=1, device_id=partner(t), device_id_type=MESH)
        return carry

    lax.fori_loop(1, devices, greet, 0)
    pl.semaphore_wait(barrier, devices - 1)

    def copy(par, t):
        return pltpu.make_async_remote_copy(
            src_ref=gath.at[par, 0],
            dst_ref=gath.at[par, t],
            send_sem=send_sem.at[par, t],
            recv_sem=recv_sem.at[par, t],
            device_id=partner(t),
            device_id_type=MESH,
        )

    def forces(par, pos, vel):
        state = jnp.concatenate([pos, vel, mass_ref[...], jnp.zeros_like(mass_ref)], 0)
        gath[par, 0] = state

        def begin(t, carry):
            copy(par, t).start()
            return carry

        lax.fori_loop(1, devices, begin, 0)
        spread_rows(state, rows)
        sums[...] = jnp.zeros_like(sums)

        def group(g, own):
            start = g * slots

            def arrive(k):
                if not (own and k == 0):
                    copy(par, start + k).wait_recv()

            if not own:
                for k in range(slots):
                    arrive(k)
            pair_tiles(gath.at[par, pl.ds(start, slots)], rows, sums, side, slots, own, arrive)

        group(0, True)

        def later(g, carry):
            group(g, False)
            return carry

        lax.fori_loop(1, groups, later, 0)

        def finish_send(t, carry):
            copy(par, t).wait_send()
            return carry

        lax.fori_loop(1, devices, finish_send, 0)
        return finish(state, sums[: pos.shape[1], :].T, sums[pos.shape[1] :, :].T)

    pos, vel = pos_ref[...], vel_ref[...]
    step_sq = time_step * time_step
    accel, jerk = forces(0, pos, vel)
    opos_ref[...] = pos
    ovel_ref[...] = vel
    oacc_ref[...] = accel
    ojerk_ref[...] = jerk

    def step(index, carry):
        position, velocity = opos_ref[...], ovel_ref[...]
        accel, jerk = oacc_ref[...], ojerk_ref[...]
        predicted_pos = (
            position
            + time_step * velocity
            + step_sq / 2.0 * accel
            + step_sq * time_step / 6.0 * jerk
        )
        predicted_vel = velocity + time_step * accel + step_sq / 2.0 * jerk
        new_accel, new_jerk = forces((index + 1) % 2, predicted_pos, predicted_vel)
        new_velocity = (
            velocity + time_step / 2.0 * (accel + new_accel) + step_sq / 12.0 * (jerk - new_jerk)
        )
        opos_ref[...] = (
            position
            + time_step / 2.0 * (velocity + new_velocity)
            + step_sq / 12.0 * (accel - new_accel)
        )
        ovel_ref[...] = new_velocity
        oacc_ref[...] = new_accel
        ojerk_ref[...] = new_jerk
        return carry

    lax.fori_loop(0, STEPS, step, 0)


def per_device(axes, sizes, position, velocity, mass):
    n = position.shape[1]
    devices = sizes[0] * sizes[1]
    depth = 2 * min(GROUP, devices) * n
    vmem = pl.BlockSpec(memory_space=pltpu.VMEM)
    shape = jax.ShapeDtypeStruct(position.shape, jnp.float32)
    return tuple(
        pl.pallas_call(
            functools.partial(kernel, axes, sizes),
            out_shape=(shape,) * 4,
            in_specs=[vmem] * 3,
            out_specs=(vmem,) * 4,
            scratch_shapes=[
                pltpu.VMEM((2, devices, 8, n), jnp.float32),
                pltpu.VMEM((6, n, LANES), jnp.float32),
                pltpu.VMEM((32, depth), jnp.bfloat16),
                pltpu.VMEM((2 * n, 32), jnp.float32),
                pltpu.SemaphoreType.DMA((2, devices)),
                pltpu.SemaphoreType.DMA((2, devices)),
            ],
            compiler_params=pltpu.CompilerParams(
                collective_id=0, has_side_effects=True, vmem_limit_bytes=40 * 1024 * 1024
            ),
        )(position, velocity, mass[None, :])
    )


def solution(mesh):
    axes = ("ia", "ja")
    sizes = (mesh.shape["ia"], mesh.shape["ja"])
    split = P(None, axes)
    return jax.shard_map(
        functools.partial(per_device, axes, sizes),
        mesh=mesh,
        in_specs=(split, split, P(axes)),
        out_specs=(split,) * 4,
        check_vma=False,
    )
```
